32 devices in a mesh: tile: 8 (over z, y), src: 4 (over x, core).
Axes of the slice: x: 2, y: 2, z: 4, core: 2. Of those that a mesh axis runs over, the one named last changes fastest.
Arguments:
- tile_tokens: bfloat16 [8192, 2048], P(('tile', 'src')), may hold values from -6 to 6
- norm_gain: float32 [2048], replicated, may hold values from 0.25 to 2.5
- up_weight: bfloat16 [2048, 2816], P('tile'), may hold values from -0.125 to 0.125
- down_weight: bfloat16 [2816, 2048], P('tile'), may hold values from -0.109375 to 0.109375
- head_weight: bfloat16 [2048, 768], P(None, 'src'), may hold values from -0.125 to 0.125
- source_index: int32 [32, 2], replicated, may hold values from 0 to 96, as said below
- source_cutoff: int32 [32], replicated, may hold values from 8 to 16
- source_weight: float32 [32], replicated, may hold values from 0.3 to 3
Outputs:
- intensity: float32 [32, 4096], P(('tile', 'src'))
The draws below stay inside these ranges and needn't reach their ends.
Inputs may be any that keep to these rules, and one draw needn't show every extreme that they name: `source_index`: in each aligned group of 4 source points the first has the least value of the group in both coordinates, the second lies exactly 32 beyond it in both, and every other lies within 32 of the first in both.
All inputs are finite; a program needn't handle non-finite values.
Results may differ from the reference program's by a relative error of at most 0.0007.
Values may be sent and summed in bfloat16 or wider, within the bound.
A program may use at most 128 MiB of HBM per device.

```python
import math
import jax
import jax.numpy as jnp
from jax import lax

D = 2048
FF = 2816
GRID = 16
SUB = 8
W = 32
REG = 64
PIX = 64
SRC_DEV = 4
PATCH = 256
ORD = 128
HEADW = 768
TOKENS = 8192
SOURCES = 32


def draw_source_index(key, part):
    group_count = SOURCES // SRC_DEV
    key_one, key_two, key_three, key_four = jax.random.split(key, 4)
    anchor = jax.random.randint(key_one, (group_count, 2), 0, ORD - REG + 1)
    top_group = jax.random.randint(key_two, (2,), 0, group_count)
    low_group = (top_group + 1 + jax.random.randint(key_three, (2,), 0, max(group_count - 1, 1))) % group_count
    group_rows = jnp.arange(group_count, dtype=jnp.int32)[:, None]
    anchor = jnp.where(group_rows == top_group[None, :], ORD - REG, anchor)
    anchor = jnp.where(group_rows == low_group[None, :], 0, anchor)
    span_width = REG - W
    offsets = jax.random.randint(key_four, (group_count, SRC_DEV, 2), 0, span_width + 1)
    member = jnp.arange(SRC_DEV, dtype=jnp.int32)[None, :, None]
    offsets = jnp.where(member == 0, 0, jnp.where(member == 1, span_width, offsets))
    return (anchor[:, None, :] + offsets).reshape(SOURCES, 2).astype(jnp.int32)


def plant(result, rng, least, largest):
    index_at = [jax.random.randint(jax.random.fold_in(rng, axis), (), 0, length) for axis, length in enumerate(result.shape)]
    main_axis = result.shape.index(max(result.shape))
    next_to = index_at[:main_axis] + [(index_at[main_axis] + 1) % result.shape[main_axis]] + index_at[main_axis + 1:]
    return result.at[tuple(index_at)].set(least).at[tuple(next_to)].set(largest)


def block_levels(own_key, dims, cuts, least, top_value):
    def one(axis_at, shards_of):
        steps = jax.random.uniform(jax.random.fold_in(jax.random.fold_in(own_key, 6), axis_at), (shards_of,), jnp.float32, least / len(cuts), top_value / len(cuts))
        return jnp.repeat(jnp.exp(steps), dims[axis_at] // shards_of).reshape((-1,) + (1,) * (len(dims) - axis_at - 1))

    factor_of = one(*cuts[0])
    for cut in cuts[1:]:
        factor_of = factor_of * one(*cut)
    return factor_of


def gaussian(key, dims, scale, most, shards=(), kind=jnp.bfloat16):
    values = scale * jax.random.normal(key, dims, jnp.float32)
    if shards:
        values = values * block_levels(key, dims, shards, -0.22, 0.18)
    return jnp.clip(values, -most, most).astype(kind)


def setup_inputs(seed: int = 0) -> dict:
    arg_keys = jax.random.split(jax.random.key(seed), 9)
    tile_tokens = gaussian(arg_keys[0], (TOKENS, D), 1.0, 6.0, ((0, 32),))
    norm_gain = jnp.clip(jnp.exp(jax.random.uniform(arg_keys[1], (D,), jnp.float32, math.log(0.25), math.log(2.5))), 0.25, 2.5)
    up_weight = gaussian(arg_keys[2], (D, FF), D ** -0.5, 0.125, ((0, 8),))
    down_weight = gaussian(arg_keys[3], (FF, D), FF ** -0.5, 0.109375, ((0, 8),))
    head_weight = gaussian(arg_keys[4], (D, HEADW), D ** -0.5, 0.125, ((1, 4),))
    source_index = draw_source_index(jax.random.fold_in(arg_keys[8], 71), 0)
    source_cutoff = plant(jax.random.randint(arg_keys[6], (SOURCES,), W // 4, W // 2 + 1), jax.random.fold_in(arg_keys[6], 1), W // 4, (W // 2 + 1) - 1).astype(jnp.int32)
    source_weight = jnp.clip(jnp.exp(jax.random.uniform(arg_keys[7], (SOURCES,), jnp.float32, math.log(0.3), math.log(3.0))), 0.3, 3.0)
    return dict(tile_tokens=tile_tokens, norm_gain=norm_gain, up_weight=up_weight, down_weight=down_weight, head_weight=head_weight, source_index=source_index, source_cutoff=source_cutoff, source_weight=source_weight)


def dft_tables():
    frequency = jnp.arange(W, dtype=jnp.int32) - W // 2
    position = jnp.arange(PIX, dtype=jnp.int32)
    phase_turns = jnp.mod(frequency[:, None] * position[None, :], PIX).astype(jnp.float32)
    phase_angle = phase_turns * (2.0 * math.pi / PIX)
    cosine = jnp.cos(phase_angle)
    sine_table = jnp.sin(phase_angle)
    table_one = jnp.concatenate([jnp.concatenate([cosine, sine_table], 1), jnp.concatenate([-sine_table, cosine], 1)], 0)
    table_two = jnp.concatenate([jnp.concatenate([cosine.T, -sine_table.T], 1), jnp.concatenate([sine_table.T, cosine.T], 1)], 0)
    return (table_one, table_two)

def pupil_mask(radius):
    frequency = jnp.arange(W, dtype=jnp.int32) - W // 2
    distance = frequency[:, None] * frequency[:, None] + frequency[None, :] * frequency[None, :]
    return (distance <= radius * radius).astype(jnp.bfloat16)

def source_power(window, table_one, table_two):
    tile_count = window.shape[0]
    split_parts = window.reshape(tile_count, 6, 2, W, W).transpose(0, 1, 3, 2, 4).reshape(tile_count, 6, W, 2 * W)
    half_field = jnp.einsum('bcik,ky->bciy', split_parts.astype(jnp.float32), table_one, precision=lax.Precision.HIGHEST)
    half_field = half_field.reshape(tile_count, 6, W, 2, PIX).transpose(0, 1, 3, 2, 4).reshape(tile_count, 6, 2 * W, PIX)
    image_field = jnp.einsum('pk,bcky->bcpy', table_two, half_field, precision=lax.Precision.HIGHEST)
    power_map = lax.optimization_barrier(jnp.sum((image_field * image_field).reshape(tile_count, 12, PIX, PIX), axis=1))
    return power_map.reshape(tile_count, PIX * PIX)

def surrogate(token_rows, norm_gain, up_weight, down_weight, head_weight):
    residual = token_rows.astype(jnp.float32)
    mean_square = lax.optimization_barrier(jnp.mean(residual * residual, axis=1, keepdims=True))
    normed = (residual * lax.rsqrt(mean_square + 1e-05) * norm_gain).astype(jnp.bfloat16)
    hidden = jax.nn.gelu(jnp.dot(normed, up_weight, preferred_element_type=jnp.float32)).astype(jnp.bfloat16)
    mixed = (residual + jnp.dot(hidden, down_weight, preferred_element_type=jnp.float32)).astype(jnp.bfloat16)
    return jnp.dot(mixed, head_weight, preferred_element_type=jnp.float32).astype(jnp.bfloat16)

def reference(tile_tokens, norm_gain, up_weight, down_weight, head_weight, source_index, source_cutoff, source_weight):
    tile_count = tile_tokens.shape[0] // PATCH

    def one_tile(token_rows):
        return surrogate(token_rows, norm_gain, up_weight, down_weight, head_weight)
    coeffs = lax.map(one_tile, tile_tokens.reshape(tile_count, PATCH, D))
    spectra = coeffs.reshape(tile_count, GRID, GRID, 12, SUB, SUB).transpose(0, 3, 1, 4, 2, 5).reshape(tile_count, 12, ORD, ORD)
    table_one, table_two = dft_tables()
    anchor_zero = jnp.zeros((), jnp.int32)

    def add_source(running, source_item):
        corner_at, radius, weight = source_item
        corner_at = corner_at.astype(jnp.int32)
        window = lax.dynamic_slice(spectra, (anchor_zero, anchor_zero, corner_at[0], corner_at[1]), (tile_count, 12, W, W)) * pupil_mask(radius)
        return (running + weight * source_power(window, table_one, table_two), None)
    running = jnp.zeros((tile_count, PIX * PIX), jnp.float32)
    image_sum, unused = lax.scan(add_source, running, (source_index, source_cutoff, source_weight))
    return image_sum * (1.0 / (6.0 * W * W * source_weight.shape[0]))
```

```python
import functools

import jax
import jax.numpy as jnp
import ml_dtypes
import numpy as np
from jax import lax
from jax.experimental import pallas as pl
from jax.experimental.pallas import tpu as pltpu
from jax.sharding import PartitionSpec as P

GRID = 16
SUB = 8
W = 32
PIX = 64
PATCH = 256
ORD = 128
HEADW = 768


def split_two(table):
    high = table.astype(ml_dtypes.bfloat16)
    low = (table - high.astype(np.float64)).astype(ml_dtypes.bfloat16)
    return high, low


def image_tables():
    angle = 2 * np.pi * (np.outer(np.arange(ORD), np.arange(PIX)) % PIX) / PIX
    c, s = np.cos(angle), np.sin(angle)
    one = np.block([[c, s, -s, c], [-s, c, -c, -s]])
    table_one = np.concatenate(split_two(one), 1)
    angle = 2 * np.pi * (np.outer(np.arange(PIX), np.arange(W)) % PIX) / PIX
    high, low = split_two(np.concatenate([np.cos(angle), np.sin(angle)], 1))
    table_two = np.concatenate([high, low, high], 1)
    spread = np.zeros((2 * SUB, SUB, 2 * SUB, GRID, SUB), ml_dtypes.bfloat16)
    for cu in range(2 * SUB):
        for v in range(SUB):
            spread[cu, v, cu, :, v] = 1
    spread = spread.reshape(2 * SUB * SUB, 2 * SUB * ORD)
    gather = np.repeat(np.eye(GRID), GRID, 1).astype(ml_dtypes.bfloat16)
    return spread, gather, table_one, table_two


def image_kernel(
    sources, index_ref, cutoff_ref, weight_ref, coeffs_ref, spread_ref, gather_ref,
    one_ref, two_ref, out_ref, spectra,
):
    row = lax.broadcasted_iota(jnp.int32, (PATCH, 2 * SUB * ORD), 0)
    lane = lax.broadcasted_iota(jnp.int32, (PATCH, 2 * SUB * ORD), 1)
    own = (row % GRID) == ((lane % ORD) // SUB)
    for pair in range(6):
        wide = jnp.dot(
            coeffs_ref[:, pair * 128:(pair + 1) * 128], spread_ref[...],
            preferred_element_type=jnp.float32,
        )
        kept = jnp.where(own, wide, 0.0).astype(jnp.bfloat16)
        rows = jnp.dot(gather_ref[...], kept, preferred_element_type=jnp.float32)
        for part in range(2):
            for u in range(SUB):
                at = (part * SUB + u) * ORD
                spectra[2 * pair + part, pl.ds(u, GRID, stride=SUB), :] = rows[:, at:at + ORD]

    order_i = lax.broadcasted_iota(jnp.int32, (W, ORD), 0) - W // 2
    order_j = lax.broadcasted_iota(jnp.int32, (W, ORD), 1) - W // 2

    def add_source(s, total):
        x0 = index_ref[2 * s]
        y0 = index_ref[2 * s + 1]
        radius = cutoff_ref[s]
        col = order_j - y0
        inside = (order_i * order_i + col * col <= radius * radius) & (col < W // 2)
        window = spectra[:, pl.ds(x0, W), :]
        window = jnp.where(inside[None], window, 0.0)
        both = jnp.concatenate(
            [jnp.concatenate([window[2 * k], window[2 * k + 1]], 1) for k in range(6)], 0
        ).astype(jnp.bfloat16)
        half = jnp.dot(both, one_ref[...], preferred_element_type=jnp.float32)
        half = half[:, :256] + half[:, 256:]
        high = half.astype(jnp.bfloat16)
        low = (half - high.astype(jnp.float32)).astype(jnp.bfloat16)

        def stacked(part):
            return jnp.concatenate(
                [
                    jnp.concatenate(
                        [part[k * W:(k + 1) * W, :128], part[k * W:(k + 1) * W, 128:]], 0
                    )
                    for k in range(6)
                ],
                1,
            )

        high, low = stacked(high), stacked(low)
        field = jnp.dot(
            two_ref[...], jnp.concatenate([high, high, low], 0),
            preferred_element_type=jnp.float32,
        )
        field = field * field
        power = field[:, :128]
        for k in range(1, 6):
            power = power + field[:, k * 128:(k + 1) * 128]
        return total + weight_ref[s] * power

    total = lax.fori_loop(0, sources, add_source, jnp.zeros((PIX, 128), jnp.float32), unroll=4)
    out_ref[...] = (total[:, :PIX] + total[:, PIX:]) * (1.0 / (6.0 * W * W * sources))


def image(coeffs, source_index, source_cutoff, source_weight):
    sources = source_weight.shape[0]
    smem = pl.BlockSpec(memory_space=pltpu.SMEM)
    vmem = pl.BlockSpec(memory_space=pltpu.VMEM)
    tables = [jnp.asarray(t) for t in image_tables()]
    out = pl.pallas_call(
        functools.partial(image_kernel, sources),
        out_shape=jax.ShapeDtypeStruct((PIX, PIX), jnp.float32),
        in_specs=[smem] * 3 + [vmem] * 5,
        out_specs=vmem,
        scratch_shapes=[pltpu.VMEM((12, ORD, ORD), jnp.float32)],
        compiler_params=pltpu.CompilerParams(vmem_limit_bytes=48 * 1024 * 1024),
        name="image_kernel",
    )(source_index.reshape(-1), source_cutoff, source_weight, coeffs, *tables)
    return out.reshape(1, PIX * PIX)


def local(
    tile_tokens, norm_gain, up_weight, down_weight, head_weight,
    source_index, source_cutoff, source_weight,
):
    groups = lax.axis_size("src")
    mine = lax.axis_index("src")
    ff = up_weight.shape[1]
    quarter = ff // groups
    folded = jnp.dot(
        down_weight, head_weight, preferred_element_type=jnp.float32
    ).astype(jnp.bfloat16)
    folded = lax.all_gather(folded, "src", axis=1, tiled=True)
    folded = lax.all_gather(folded, "tile", axis=0, tiled=True)
    folded = lax.dynamic_slice_in_dim(folded, mine * quarter, quarter, 0)
    up = lax.dynamic_slice_in_dim(up_weight, mine * quarter, quarter, 1)
    up = lax.all_gather(up, "tile", axis=0, tiled=True)
    tokens = lax.all_gather(tile_tokens, "src", axis=0, tiled=True)
    residual = tokens.astype(jnp.float32)
    mean_square = jnp.mean(residual * residual, axis=1, keepdims=True)
    normed = (residual * lax.rsqrt(mean_square + 1e-05) * norm_gain).astype(jnp.bfloat16)
    hidden = jax.nn.gelu(
        jnp.dot(normed, up, preferred_element_type=jnp.float32)
    ).astype(jnp.bfloat16)
    part = jnp.dot(hidden, folded, preferred_element_type=jnp.float32)
    kept = jnp.dot(tokens, head_weight, preferred_element_type=jnp.float32)
    part = lax.dynamic_update_slice_in_dim(
        part,
        lax.dynamic_slice_in_dim(part, mine * kept.shape[1], kept.shape[1], 1) + kept,
        mine * kept.shape[1], 1,
    )
    coeffs = lax.psum_scatter(part, "src", scatter_dimension=0, tiled=True).astype(jnp.bfloat16)
    return image(coeffs, source_index, source_cutoff, source_weight)


def solution(mesh):
    return jax.shard_map(
        local,
        mesh=mesh,
        in_specs=(
            P(("tile", "src"), None), P(), P("tile", None), P("tile", None),
            P(None, "src"), P(), P(), P(),
        ),
        out_specs=P(("tile", "src"), None),
        check_vma=False,
    )
```

```python
import functools

import jax
import jax.numpy as jnp
import ml_dtypes
import numpy as np
from jax import lax
from jax.experimental import pallas as pl
from jax.experimental.pallas import tpu as pltpu
from jax.sharding import PartitionSpec as P

GRID = 16
SUB = 8
W = 32
PIX = 64
PATCH = 256
ORD = 128
HEADW = 768


def split_two(table):
    high = table.astype(ml_dtypes.bfloat16)
    low = (table - high.astype(np.float64)).astype(ml_dtypes.bfloat16)
    return high, low


def image_tables():
    angle = 2 * np.pi * (np.outer(np.arange(ORD), np.arange(PIX)) % PIX) / PIX
    c, s = np.cos(angle), np.sin(angle)
    one = np.block([[c, s, -s, c], [-s, c, -c, -s]])
    table_one = np.concatenate(split_two(one), 1)
    angle = 2 * np.pi * (np.outer(np.arange(PIX), np.arange(W)) % PIX) / PIX
    high, low = split_two(np.concatenate([np.cos(angle), np.sin(angle)], 1))
    table_two = np.concatenate([high, low, high], 1)
    spread = np.zeros((2 * SUB, SUB, 2 * SUB, GRID, SUB), ml_dtypes.bfloat16)
    for cu in range(2 * SUB):
        for v in range(SUB):
            spread[cu, v, cu, :, v] = 1
    spread = spread.reshape(2 * SUB * SUB, 2 * SUB * ORD)
    gather = np.repeat(np.eye(GRID), GRID, 1).astype(ml_dtypes.bfloat16)
    return spread, gather, table_one, table_two


def image_kernel(
    sources, index_ref, cutoff_ref, weight_ref, coeffs_ref, spread_ref, gather_ref,
    one_ref, two_ref, out_ref, spectra,
):
    row = lax.broadcasted_iota(jnp.int32, (PATCH, 2 * SUB * ORD), 0)
    lane = lax.broadcasted_iota(jnp.int32, (PATCH, 2 * SUB * ORD), 1)
    own = (row % GRID) == ((lane % ORD) // SUB)
    for pair in range(6):
        wide = jnp.dot(
            coeffs_ref[:, pair * 128:(pair + 1) * 128], spread_ref[...],
            preferred_element_type=jnp.float32,
        )
        kept = jnp.where(own, wide, 0.0).astype(jnp.bfloat16)
        rows = jnp.dot(gather_ref[...], kept, preferred_element_type=jnp.float32)
        for part in range(2):
            for u in range(SUB):
                at = (part * SUB + u) * ORD
                spectra[2 * pair + part, pl.ds(u, GRID, stride=SUB), :] = rows[:, at:at + ORD]

    order_i = lax.broadcasted_iota(jnp.int32, (W, ORD), 0) - W // 2
    order_j = lax.broadcasted_iota(jnp.int32, (W, ORD), 1) - W // 2

    def add_source(s, total):
        x0 = index_ref[2 * s]
        y0 = index_ref[2 * s + 1]
        radius = cutoff_ref[s]
        col = order_j - y0
        inside = (order_i * order_i + col * col <= radius * radius) & (col < W // 2)
        window = spectra[:, pl.ds(x0, W), :]
        window = jnp.where(inside[None], window, 0.0)
        both = jnp.concatenate(
            [jnp.concatenate([window[2 * k], window[2 * k + 1]], 1) for k in range(6)], 0
        ).astype(jnp.bfloat16)
        half = jnp.dot(both, one_ref[...], preferred_element_type=jnp.float32)
        half = half[:, :256] + half[:, 256:]
        high = half.astype(jnp.bfloat16)
        low = (half - high.astype(jnp.float32)).astype(jnp.bfloat16)

        def stacked(part):
            return jnp.concatenate(
                [
                    jnp.concatenate(
                        [part[k * W:(k + 1) * W, :128], part[k * W:(k + 1) * W, 128:]], 0
                    )
                    for k in range(6)
                ],
                1,
            )

        high, low = stacked(high), stacked(low)
        field = jnp.dot(
            two_ref[...], jnp.concatenate([high, high, low], 0),
            preferred_element_type=jnp.float32,
        )
        field = field * field
        power = field[:, :128]
        for k in range(1, 6):
            power = power + field[:, k * 128:(k + 1) * 128]
        return total + weight_ref[s] * power

    total = lax.fori_loop(0, sources, add_source, jnp.zeros((PIX, 128), jnp.float32), unroll=4)
    out_ref[...] = (total[:, :PIX] + total[:, PIX:]) * (1.0 / (6.0 * W * W * sources))


def image(coeffs, source_index, source_cutoff, source_weight):
    sources = source_weight.shape[0]
    smem = pl.BlockSpec(memory_space=pltpu.SMEM)
    vmem = pl.BlockSpec(memory_space=pltpu.VMEM)
    tables = [jnp.asarray(t) for t in image_tables()]
    out = pl.pallas_call(
        functools.partial(image_kernel, sources),
        out_shape=jax.ShapeDtypeStruct((PIX, PIX), jnp.float32),
        in_specs=[smem] * 3 + [vmem] * 5,
        out_specs=vmem,
        scratch_shapes=[pltpu.VMEM((12, ORD, ORD), jnp.float32)],
        compiler_params=pltpu.CompilerParams(vmem_limit_bytes=48 * 1024 * 1024),
        name="image_kernel",
    )(source_index.reshape(-1), source_cutoff, source_weight, coeffs, *tables)
    return out.reshape(1, PIX * PIX)


MESH = pl.DeviceIdType.MESH


def surrogate_kernel(
    tiles, groups, tok_ref, gain_ref, up_ref, down_ref, head_ref, out_ref,
    tok_buf, norm_buf, up_buf, acc, block, block_in, fold_own, fold_buf, fold_all,
    part, mine_part, sib_buf, cross_out, cross_in,
    up_send, up_fsend, up_recv, tok_send, tok_fsend, tok_recv, block_send, block_recv,
    fold_send, fold_fsend, fold_recv, sib_send, sib_recv, cross_send, cross_recv,
):
    t, s = lax.axis_index("tile"), lax.axis_index("src")
    tile_pairs, chips = tiles // 2, groups // 2
    side, pair = lax.rem(t, 2), t // 2
    core, chip = lax.rem(s, 2), s // 2
    width = head_ref.shape[1]
    depth = up_ref.shape[0]
    share = tiles // groups
    owner = t // share

    def send(source, target, sent, got, tile, col):
        return pltpu.make_async_remote_copy(
            src_ref=source, dst_ref=target, send_sem=sent, recv_sem=got,
            device_id={"tile": tile, "src": col}, device_id_type=MESH,
        )

    def tile_at(k):
        return 2 * lax.rem(pair + k, tile_pairs) + side

    def col_at(k):
        return 2 * lax.rem(chip + k, chips) + core

    tile_mate = t + 1 - 2 * side
    col_mate = s + 1 - 2 * core

    barrier = pltpu.get_barrier_semaphore()
    for k in range(1, tile_pairs):
        pl.semaphore_signal(barrier, inc=1, device_id={"tile": tile_at(k), "src": s}, device_id_type=MESH)
    pl.semaphore_signal(barrier, inc=1, device_id={"tile": tile_mate, "src": s}, device_id_type=MESH)
    for k in range(1, groups):
        pl.semaphore_signal(
            barrier, inc=1, device_id={"tile": t, "src": lax.rem(s + k, groups)}, device_id_type=MESH
        )
    pl.semaphore_wait(barrier, tile_pairs + groups - 1)

    up_copies = [
        send(up_ref, up_buf.at[t], up_send.at[k], up_recv.at[t], tile_mate if k == 0 else tile_at(k), s)
        for k in range(tile_pairs)
    ]
    tok_copies = [
        send(tok_ref, tok_buf.at[s], tok_send.at[k], tok_recv.at[s], t, col_mate if k == 0 else col_at(k))
        for k in range(chips)
    ]
    for copy in tok_copies[1:] + up_copies[1:] + tok_copies[:1] + up_copies[:1]:
        copy.start()

    block[...] = jnp.dot(
        down_ref[...], head_ref[...], preferred_element_type=jnp.float32
    ).astype(jnp.bfloat16)
    block_copy = send(block, block_in.at[s], block_send, block_recv.at[s], t, owner)

    @pl.when(s != owner)
    def _():
        block_copy.start()

    def normalise(source, col):
        value = source[...].astype(jnp.float32)
        square = jnp.mean(value * value, axis=1, keepdims=True)
        value = (value * lax.rsqrt(square + 1e-05) * gain_ref[...]).astype(jnp.bfloat16)
        for j in range(tiles):
            norm_buf[j, col] = value[:, j * depth:(j + 1) * depth]

    normalise(tok_ref, s)

    def fold_copy(k):
        return send(
            fold_own, fold_buf.at[lax.rem(t, share)], fold_send.at[k],
            fold_recv.at[lax.rem(t, share)], tile_mate if k == 0 else tile_at(k), s,
        )

    @pl.when(s == owner)
    def _():
        for k in range(1, groups):
            col = lax.rem(s + k, groups)
            send(block, block_in.at[col], block_send, block_recv.at[col], t, s).wait_recv()
        for q in range(groups):
            @pl.when(s == q)
            def _():
                fold_own[:, q * width:(q + 1) * width] = block[...]

            @pl.when(s != q)
            def _():
                fold_own[:, q * width:(q + 1) * width] = block_in[q]

        for k in range(tile_pairs):
            fold_copy(k).start()
        fold_buf[lax.rem(t, share)] = fold_own[...]

    def up_forward(k):
        at = tile_at(k)
        return send(up_buf.at[at], up_buf.at[at], up_fsend.at[k], up_recv.at[at], tile_mate, s)

    def fold_forward(j):
        at = 2 * j + side
        return send(fold_buf.at[at], fold_buf.at[at], fold_fsend.at[j], fold_recv.at[at], tile_mate, s)

    def fold_is_mine(j):
        return pair == s * (share // 2) + j

    def tok_forward(k):
        at = col_at(k)
        return send(tok_buf.at[at], tok_buf.at[at], tok_fsend.at[k], tok_recv.at[at], t, col_mate)

    for k in range(1, tile_pairs):
        up_forward(k).wait_recv()
        up_forward(k).start()
        if k == 1:
            send(
                tok_ref, tok_buf.at[col_mate], tok_send.at[0], tok_recv.at[col_mate], t, col_mate
            ).wait_recv()
            normalise(tok_buf.at[col_mate], col_mate)
    for j in range(share // 2):
        @pl.when(jnp.logical_not(fold_is_mine(j)))
        def _():
            fold_forward(j).wait_recv()
            fold_forward(j).start()
    for k in range(1, chips):
        tok_forward(k).wait_recv()
        tok_forward(k).start()
    for k in range(1, chips):
        normalise(tok_buf.at[col_at(k)], col_at(k))
    for k in range(1, chips):
        at = 2 * lax.rem(chip + k, chips) + 1 - core
        send(tok_ref, tok_buf.at[at], tok_send.at[0], tok_recv.at[at], t, col_mate).wait_recv()
        normalise(tok_buf.at[at], at)

    def add_block(rows_ref, at, first=False):
        def step(g, carry):
            value = jnp.dot(norm_buf[at, g], rows_ref[...], preferred_element_type=jnp.float32)
            if first:
                acc[g] = value
            else:
                acc[g] = acc[g] + value
            return carry
        lax.fori_loop(0, groups, step, 0)

    add_block(up_ref, t, True)
    for k in range(1, tile_pairs):
        add_block(up_buf.at[tile_at(k)], tile_at(k))
    for k in range(tile_pairs):
        at = 2 * lax.rem(pair + k, tile_pairs) + 1 - side
        send(up_ref, up_buf.at[at], up_send.at[0], up_recv.at[at], tile_mate, s).wait_recv()
        add_block(up_buf.at[at], at)
    for j in range(share // 2):
        at = 2 * j + 1 - side
        send(fold_own, fold_buf.at[at], fold_send.at[0], fold_recv.at[at], tile_mate, s).wait_recv()
    folded = jnp.concatenate([fold_buf[j].astype(jnp.float32) for j in range(share)], 0)
    real = folded.shape[0]
    fold_all[...] = jnp.zeros_like(fold_all)
    fold_all[:real, :] = folded.astype(jnp.bfloat16)

    def partial(col, target):
        value = acc[col]
        inner = 0.7978845608028654 * (value + 0.044715 * (value * value * value))
        hidden = (0.5 * value * (1.0 + jnp.tanh(inner))).astype(jnp.bfloat16)
        target[...] = jnp.dot(hidden, fold_all[...], preferred_element_type=jnp.float32)

        def keep(source):
            kept = jnp.dot(source[...], head_ref[...], preferred_element_type=jnp.float32)
            for q in range(groups):
                @pl.when(s == q)
                def _():
                    target[:, q * width:(q + 1) * width] += kept

        keep(tok_buf.at[col])

    tok_buf[s] = tok_ref[...]

    def sib_copy(k):
        return send(part.at[k], sib_buf.at[k], sib_send.at[k], sib_recv.at[k], t, col_mate)

    def cross_copy(k):
        return send(cross_out.at[k], cross_in.at[k], cross_send.at[k], cross_recv.at[k], t, col_at(k))

    for k in list(range(1, chips)) + [0]:
        partial(2 * lax.rem(chip + k, chips) + 1 - core, part.at[k])
        sib_copy(k).start()
        partial(col_at(k), mine_part)
        sib_copy(k).wait_recv()
        mine_part[...] += sib_buf[k]
        if k > 0:
            cross_out[k] = mine_part[...].astype(jnp.bfloat16)
            cross_copy(k).start()
    total = mine_part[...]
    for k in range(1, chips):
        cross_copy(k).wait_recv()
        total = total + cross_in[k].astype(jnp.float32)
    out_ref[...] = total.astype(jnp.bfloat16)

    for copy in up_copies + tok_copies:
        copy.wait_send()
    for k in range(1, tile_pairs):
        up_forward(k).wait_send()
    for k in range(1, chips):
        tok_forward(k).wait_send()
        cross_copy(k).wait_send()
    for k in range(chips):
        sib_copy(k).wait_send()

    @pl.when(s != owner)
    def _():
        block_copy.wait_send()

    @pl.when(s == owner)
    def _():
        for k in range(tile_pairs):
            fold_copy(k).wait_send()

    for j in range(share // 2):
        @pl.when(jnp.logical_not(fold_is_mine(j)))
        def _():
            fold_forward(j).wait_send()


def surrogate(tokens, gain, up, down, head, tiles, groups):
    rows, model = tokens.shape
    depth, wide = up.shape
    ff_rows, width = down.shape[0], head.shape[1]
    outs = groups * width
    share, chips = tiles // groups, groups // 2
    dma = pltpu.SemaphoreType.DMA
    bf16, f32 = jnp.bfloat16, jnp.float32
    vmem = pl.BlockSpec(memory_space=pltpu.VMEM)
    return pl.pallas_call(
        functools.partial(surrogate_kernel, tiles, groups),
        out_shape=jax.ShapeDtypeStruct((rows, outs), bf16),
        in_specs=[vmem] * 5,
        out_specs=vmem,
        scratch_shapes=[
            pltpu.VMEM((groups, rows, model), bf16),
            pltpu.VMEM((tiles, groups, rows, depth), bf16),
            pltpu.VMEM((tiles, depth, wide), bf16),
            pltpu.VMEM((groups, rows, wide), f32),
            pltpu.VMEM((ff_rows, width), bf16),
            pltpu.VMEM((groups, ff_rows, width), bf16),
            pltpu.VMEM((ff_rows, outs), bf16),
            pltpu.VMEM((share, ff_rows, outs), bf16),
            pltpu.VMEM((wide, outs), bf16),
            pltpu.VMEM((chips, rows, outs), f32),
            pltpu.VMEM((rows, outs), f32),
            pltpu.VMEM((chips, rows, outs), f32),
            pltpu.VMEM((chips, rows, outs), bf16),
            pltpu.VMEM((chips, rows, outs), bf16),
            dma((tiles // 2,)), dma((tiles // 2,)), dma((tiles,)),
            dma((chips,)), dma((chips,)), dma((groups,)),
            dma(()), dma((groups,)),
            dma((tiles // 2,)), dma((share // 2,)), dma((share,)),
            dma((chips,)), dma((chips,)), dma((chips,)), dma((chips,)),
        ],
        compiler_params=pltpu.CompilerParams(
            collective_id=0, has_side_effects=True, vmem_limit_bytes=52 * 1024 * 1024
        ),
        name="surrogate_kernel",
    )(tokens, gain.reshape(1, -1), up, down, head)


def local(
    tile_tokens, norm_gain, up_weight, down_weight, head_weight,
    source_index, source_cutoff, source_weight,
):
    groups = lax.axis_size("src")
    mine = lax.axis_index("src")
    ff = up_weight.shape[1]
    quarter = ff // groups
    wide = -(-quarter // 256) * 256
    up = lax.dynamic_slice_in_dim(up_weight, mine * quarter, quarter, 1)
    up = jnp.pad(up, ((0, 0), (0, wide - quarter)))
    coeffs = surrogate(
        tile_tokens, norm_gain, up, down_weight, head_weight, lax.axis_size("tile"), groups
    )
    return image(coeffs, source_index, source_cutoff, source_weight)


def solution(mesh):
    return jax.shard_map(
        local,
        mesh=mesh,
        in_specs=(
            P(("tile", "src"), None), P(), P("tile", None), P("tile", None),
            P(None, "src"), P(), P(), P(),
        ),
        out_specs=P(("tile", "src"), None),
        check_vma=False,
    )
```

```python
import functools

import jax
import jax.numpy as jnp
import ml_dtypes
import numpy as np
from jax import lax
from jax.experimental import pallas as pl
from jax.experimental.pallas import tpu as pltpu
from jax.sharding import PartitionSpec as P

GRID = 16
SUB = 8
W = 32
PIX = 64
PATCH = 256
ORD = 128
HEADW = 768


def split_two(table):
    high = table.astype(ml_dtypes.bfloat16)
    low = (table - high.astype(np.float64)).astype(ml_dtypes.bfloat16)
    return high, low


def image_tables():
    angle = 2 * np.pi * (np.outer(np.arange(ORD), np.arange(PIX)) % PIX) / PIX
    c, s = np.cos(angle), np.sin(angle)
    one = np.block([[c, s, -s, c], [-s, c, -c, -s]])
    table_one = np.concatenate(split_two(one), 1)
    angle = 2 * np.pi * (np.outer(np.arange(PIX), np.arange(W)) % PIX) / PIX
    high, low = split_two(np.concatenate([np.cos(angle), np.sin(angle)], 1))
    table_two = np.concatenate([high, low, high], 1)
    spread = np.zeros((2 * SUB, SUB, 2 * SUB, GRID, SUB), ml_dtypes.bfloat16)
    for cu in range(2 * SUB):
        for v in range(SUB):
            spread[cu, v, cu, :, v] = 1
    spread = spread.reshape(2 * SUB * SUB, 2 * SUB * ORD)
    gather = np.repeat(np.eye(GRID), GRID, 1).astype(ml_dtypes.bfloat16)
    return spread, gather, table_one, table_two


def image_kernel(
    sources, index_ref, cutoff_ref, weight_ref, coeffs_ref, spread_ref, gather_ref,
    one_ref, two_ref, out_ref, spectra,
):
    row = lax.broadcasted_iota(jnp.int32, (PATCH, 2 * SUB * ORD), 0)
    lane = lax.broadcasted_iota(jnp.int32, (PATCH, 2 * SUB * ORD), 1)
    own = (row % GRID) == ((lane % ORD) // SUB)
    for pair in range(6):
        wide = jnp.dot(
            coeffs_ref[:, pair * 128:(pair + 1) * 128], spread_ref[...],
            preferred_element_type=jnp.float32,
        )
        kept = jnp.where(own, wide, 0.0).astype(jnp.bfloat16)
        rows = jnp.dot(gather_ref[...], kept, preferred_element_type=jnp.float32)
        for part in range(2):
            for u in range(SUB):
                at = (part * SUB + u) * ORD
                spectra[2 * pair + part, pl.ds(u, GRID, stride=SUB), :] = rows[:, at:at + ORD]

    order_i = lax.broadcasted_iota(jnp.int32, (W, ORD), 0) - W // 2
    order_j = lax.broadcasted_iota(jnp.int32, (W, ORD), 1) - W // 2

    def add_source(s, total):
        x0 = index_ref[2 * s]
        y0 = index_ref[2 * s + 1]
        radius = cutoff_ref[s]
        col = order_j - y0
        inside = (order_i * order_i + col * col <= radius * radius) & (col < W // 2)
        window = spectra[:, pl.ds(x0, W), :]
        window = jnp.where(inside[None], window, 0.0)
        both = jnp.concatenate(
            [jnp.concatenate([window[2 * k], window[2 * k + 1]], 1) for k in range(6)], 0
        ).astype(jnp.bfloat16)
        half = jnp.dot(both, one_ref[...], preferred_element_type=jnp.float32)
        half = half[:, :256] + half[:, 256:]
        high = half.astype(jnp.bfloat16)
        low = (half - high.astype(jnp.float32)).astype(jnp.bfloat16)

        def stacked(part):
            return jnp.concatenate(
                [
                    jnp.concatenate(
                        [part[k * W:(k + 1) * W, :128], part[k * W:(k + 1) * W, 128:]], 0
                    )
                    for k in range(6)
                ],
                1,
            )

        high, low = stacked(high), stacked(low)
        field = jnp.dot(
            two_ref[...], jnp.concatenate([high, high, low], 0),
            preferred_element_type=jnp.float32,
        )
        field = field * field
        power = field[:, :128]
        for k in range(1, 6):
            power = power + field[:, k * 128:(k + 1) * 128]
        return total + weight_ref[s] * power

    total = lax.fori_loop(0, sources, add_source, jnp.zeros((PIX, 128), jnp.float32), unroll=4)
    out_ref[...] = (total[:, :PIX] + total[:, PIX:]) * (1.0 / (6.0 * W * W * sources))


def image(coeffs, source_index, source_cutoff, source_weight):
    sources = source_weight.shape[0]
    smem = pl.BlockSpec(memory_space=pltpu.SMEM)
    vmem = pl.BlockSpec(memory_space=pltpu.VMEM)
    tables = [jnp.asarray(t) for t in image_tables()]
    out = pl.pallas_call(
        functools.partial(image_kernel, sources),
        out_shape=jax.ShapeDtypeStruct((PIX, PIX), jnp.float32),
        in_specs=[smem] * 3 + [vmem] * 5,
        out_specs=vmem,
        scratch_shapes=[pltpu.VMEM((12, ORD, ORD), jnp.float32)],
        compiler_params=pltpu.CompilerParams(vmem_limit_bytes=24 * 1024 * 1024),
        name="image_kernel",
    )(source_index.reshape(-1), source_cutoff, source_weight, coeffs, *tables)
    return out.reshape(1, PIX * PIX)


MESH = pl.DeviceIdType.MESH


def surrogate_kernel(
    tiles, groups, tok_ref, gain_ref, up_ref, down_ref, head_ref, out_ref,
    tok_buf, norm_buf, up_buf, acc, block, block_in, fold_own, fold_buf, fold_all,
    part, mine_part, sib_buf, cross_out, cross_in, kept_buf,
    up_send, up_fsend, up_lsend, up_recv, tok_send, tok_fsend, tok_recv, block_send, block_recv,
    fold_send, fold_fsend, fold_lsend, fold_recv, sib_send, sib_recv, cross_send, cross_recv,
):
    t, s = lax.axis_index("tile"), lax.axis_index("src")
    tile_pairs, chips = tiles // 2, groups // 2
    side, pair = lax.rem(t, 2), t // 2
    core, chip = lax.rem(s, 2), s // 2
    width = head_ref.shape[1]
    depth = up_ref.shape[0]
    share = tiles // groups
    owner = t // share

    def send(source, target, sent, got, tile, col):
        return pltpu.make_async_remote_copy(
            src_ref=source, dst_ref=target, send_sem=sent, recv_sem=got,
            device_id={"tile": tile, "src": col}, device_id_type=MESH,
        )

    def tile_at(k):
        return 2 * lax.rem(pair + k, tile_pairs) + side

    def line(step):
        return (pair + step >= 0) & (pair + step < tile_pairs)

    def col_at(k):
        return 2 * lax.rem(chip + k, chips) + core

    tile_mate = t + 1 - 2 * side
    col_mate = s + 1 - 2 * core

    barrier = pltpu.get_barrier_semaphore()
    for step in (-1, 1):
        @pl.when(line(step))
        def _():
            pl.semaphore_signal(
                barrier, inc=1, device_id={"tile": t + 2 * step, "src": s}, device_id_type=MESH
            )
    pl.semaphore_signal(barrier, inc=1, device_id={"tile": tile_mate, "src": s}, device_id_type=MESH)
    for k in range(1, groups):
        pl.semaphore_signal(
            barrier, inc=1, device_id={"tile": t, "src": lax.rem(s + k, groups)}, device_id_type=MESH
        )
    pl.semaphore_wait(barrier, groups + line(-1).astype(jnp.int32) + line(1).astype(jnp.int32))

    up_mate = send(up_ref, up_buf.at[t], up_send.at[0], up_recv.at[t], tile_mate, s)
    up_line = {
        step: send(up_ref, up_buf.at[t], up_send.at[(3 + step) // 2], up_recv.at[t], t + 2 * step, s)
        for step in (-1, 1)
    }
    tok_copies = [
        send(tok_ref, tok_buf.at[s], tok_send.at[k], tok_recv.at[s], t, col_mate if k == 0 else col_at(k))
        for k in range(chips)
    ]
    for step in (-1, 1):
        @pl.when(line(step))
        def _():
            up_line[step].start()
    for copy in tok_copies[1:] + [up_mate] + tok_copies[:1]:
        copy.start()

    block[...] = jnp.dot(
        down_ref[...], head_ref[...], preferred_element_type=jnp.float32
    ).astype(jnp.bfloat16)
    block_copy = send(block, block_in.at[s], block_send, block_recv.at[s], t, owner)

    @pl.when(s != owner)
    def _():
        block_copy.start()

    def normalise(source, col):
        value = source[...].astype(jnp.float32)
        square = jnp.mean(value * value, axis=1, keepdims=True)
        value = (value * lax.rsqrt(square + 1e-05) * gain_ref[...]).astype(jnp.bfloat16)
        for j in range(tiles):
            norm_buf[j, col] = value[:, j * depth:(j + 1) * depth]

    def keep(source, col):
        kept = jnp.dot(source[...], head_ref[...], preferred_element_type=jnp.float32)
        kept_buf[col] = jnp.zeros(kept_buf.shape[1:], jnp.float32)
        for q in range(groups):
            @pl.when(s == q)
            def _():
                kept_buf[col, :, q * width:(q + 1) * width] = kept

    own_fold = lax.rem(t, share)
    fold_mate = send(
        fold_own, fold_buf.at[own_fold], fold_send.at[0], fold_recv.at[own_fold], tile_mate, s
    )
    fold_line = {
        step: send(
            fold_own, fold_buf.at[own_fold], fold_send.at[(3 + step) // 2],
            fold_recv.at[own_fold], t + 2 * step, s,
        )
        for step in (-1, 1)
    }

    @pl.when(s == owner)
    def _():
        for k in range(1, groups):
            col = lax.rem(s + k, groups)
            send(block, block_in.at[col], block_send, block_recv.at[col], t, s).wait_recv()
        for q in range(groups):
            @pl.when(s == q)
            def _():
                fold_own[:, q * width:(q + 1) * width] = block[...]

            @pl.when(s != q)
            def _():
                fold_own[:, q * width:(q + 1) * width] = block_in[q]

        for step in (-1, 1):
            @pl.when(line(step))
            def _():
                fold_line[step].start()
        fold_mate.start()
        fold_buf[lax.rem(t, share)] = fold_own[...]

    def up_forward(k, step):
        at = t - 2 * step * k
        return (
            send(up_buf.at[at], up_buf.at[at], up_fsend.at[at // 2], up_recv.at[at], tile_mate, s),
            send(up_buf.at[at], up_buf.at[at], up_lsend.at[at // 2], up_recv.at[at], t + 2 * step, s),
        )

    def fold_forward(j, step):
        at = 2 * j + side
        return (
            send(fold_buf.at[at], fold_buf.at[at], fold_fsend.at[j], fold_recv.at[at], tile_mate, s),
            send(fold_buf.at[at], fold_buf.at[at], fold_lsend.at[j], fold_recv.at[at], t + 2 * step, s),
        )

    def fold_pair(j):
        return s * (share // 2) + j

    def up_handle(k, act):
        for step in (1, -1):
            @pl.when(line(-step * k))
            def _():
                act(up_forward(k, step), step)

    def fold_handle(k, act):
        for j in range(share // 2):
            for step in (1, -1):
                @pl.when(pair == fold_pair(j) + step * k)
                def _():
                    act(fold_forward(j, step), step)

    def pass_on(copies, step):
        copies[0].wait_recv()

        @pl.when(line(step))
        def _():
            copies[1].start()
        copies[0].start()

    def finish(copies, step):
        copies[0].wait_send()

        @pl.when(line(step))
        def _():
            copies[1].wait_send()

    def tok_forward(k):
        at = col_at(k)
        return send(tok_buf.at[at], tok_buf.at[at], tok_fsend.at[k], tok_recv.at[at], t, col_mate)

    def add_block(rows_ref, at, cols, first=False):
        for g in cols:
            value = jnp.dot(norm_buf[at, g], rows_ref[...], preferred_element_type=jnp.float32)
            if first:
                acc[g] = value
            else:
                acc[g] = acc[g] + value

    near = [s, col_mate]
    normalise(tok_ref, s)
    for k in range(1, tile_pairs):
        up_handle(k, pass_on)
        if k > 1:
            fold_handle(k - 1, pass_on)
        if k == 1:
            send(
                tok_ref, tok_buf.at[col_mate], tok_send.at[0], tok_recv.at[col_mate], t, col_mate
            ).wait_recv()
            normalise(tok_buf.at[col_mate], col_mate)
            keep(tok_ref, s)
            add_block(up_ref, t, near, True)
    fold_handle(tile_pairs - 1, pass_on)
    for k in range(1, chips):
        tok_forward(k).wait_recv()
        tok_forward(k).start()
    keep(tok_buf.at[col_mate], col_mate)
    for k in range(1, chips):
        normalise(tok_buf.at[col_at(k)], col_at(k))
        keep(tok_buf.at[col_at(k)], col_at(k))
    far = []
    for k in range(1, chips):
        at = 2 * lax.rem(chip + k, chips) + 1 - core
        send(tok_ref, tok_buf.at[at], tok_send.at[0], tok_recv.at[at], t, col_mate).wait_recv()
        normalise(tok_buf.at[at], at)
        keep(tok_buf.at[at], at)
        far += [col_at(k), at]
    add_block(up_ref, t, far, True)
    for k in range(1, tile_pairs):
        add_block(up_buf.at[tile_at(k)], tile_at(k), near + far)
    for k in range(tile_pairs):
        for step in ((1, -1) if k else (1,)):
            @pl.when(line(-step * k))
            def _():
                at = tile_mate - 2 * step * k
                send(up_ref, up_buf.at[at], up_send.at[0], up_recv.at[at], tile_mate, s).wait_recv()
                add_block(up_buf.at[at], at, near + far)
    for j in range(share // 2):
        at = 2 * j + 1 - side
        send(fold_own, fold_buf.at[at], fold_send.at[0], fold_recv.at[at], tile_mate, s).wait_recv()
    folded = jnp.concatenate([fold_buf[j].astype(jnp.float32) for j in range(share)], 0)
    real = folded.shape[0]
    fold_all[...] = jnp.zeros_like(fold_all)
    fold_all[:real, :] = folded.astype(jnp.bfloat16)

    def partial(col, target):
        value = acc[col]
        inner = 0.7978845608028654 * (value + 0.044715 * (value * value * value))
        hidden = (0.5 * value * (1.0 + jnp.tanh(inner))).astype(jnp.bfloat16)
        target[...] = (
            jnp.dot(hidden, fold_all[...], preferred_element_type=jnp.float32) + kept_buf[col]
        )

    def sib_copy(k):
        return send(part.at[k], sib_buf.at[k], sib_send.at[k], sib_recv.at[k], t, col_mate)

    def cross_copy(k):
        return send(cross_out.at[k], cross_in.at[k], cross_send.at[k], cross_recv.at[k], t, col_at(k))

    for k in list(range(1, chips)) + [0]:
        partial(2 * lax.rem(chip + k, chips) + 1 - core, part.at[k])
        sib_copy(k).start()
        partial(col_at(k), mine_part)
        sib_copy(k).wait_recv()
        mine_part[...] += sib_buf[k]
        if k > 0:
            cross_out[k] = mine_part[...].astype(jnp.bfloat16)
            cross_copy(k).start()
    total = mine_part[...]
    for k in range(1, chips):
        cross_copy(k).wait_recv()
        total = total + cross_in[k].astype(jnp.float32)
    out_ref[...] = total.astype(jnp.bfloat16)

    for copy in [up_mate] + tok_copies:
        copy.wait_send()
    for step in (-1, 1):
        @pl.when(line(step))
        def _():
            up_line[step].wait_send()
    for k in range(1, tile_pairs):
        up_handle(k, finish)
        fold_handle(k, finish)
    for k in range(1, chips):
        tok_forward(k).wait_send()
        cross_copy(k).wait_send()
    for k in range(chips):
        sib_copy(k).wait_send()

    @pl.when(s != owner)
    def _():
        block_copy.wait_send()

    @pl.when(s == owner)
    def _():
        fold_mate.wait_send()
        for step in (-1, 1):
            @pl.when(line(step))
            def _():
                fold_line[step].wait_send()


def surrogate(tokens, gain, up, down, head, tiles, groups):
    rows, model = tokens.shape
    depth, wide = up.shape
    ff_rows, width = down.shape[0], head.shape[1]
    outs = groups * width
    share, chips = tiles // groups, groups // 2
    dma = pltpu.SemaphoreType.DMA
    bf16, f32 = jnp.bfloat16, jnp.float32
    vmem = pl.BlockSpec(memory_space=pltpu.VMEM)
    return pl.pallas_call(
        functools.partial(surrogate_kernel, tiles, groups),
        out_shape=jax.ShapeDtypeStruct((rows, outs), bf16),
        in_specs=[vmem] * 5,
        out_specs=vmem,
        scratch_shapes=[
            pltpu.VMEM((groups, rows, model), bf16),
            pltpu.VMEM((tiles, groups, rows, depth), bf16),
            pltpu.VMEM((tiles, depth, wide), bf16),
            pltpu.VMEM((groups, rows, wide), f32),
            pltpu.VMEM((ff_rows, width), bf16),
            pltpu.VMEM((groups, ff_rows, width), bf16),
            pltpu.VMEM((ff_rows, outs), bf16),
            pltpu.VMEM((share, ff_rows, outs), bf16),
            pltpu.VMEM((wide, outs), bf16),
            pltpu.VMEM((chips, rows, outs), f32),
            pltpu.VMEM((rows, outs), f32),
            pltpu.VMEM((chips, rows, outs), f32),
            pltpu.VMEM((chips, rows, outs), bf16),
            pltpu.VMEM((chips, rows, outs), bf16),
            pltpu.VMEM((groups, rows, outs), f32),
            dma((3,)), dma((tiles // 2,)), dma((tiles // 2,)), dma((tiles,)),
            dma((chips,)), dma((chips,)), dma((groups,)),
            dma(()), dma((groups,)),
            dma((3,)), dma((share // 2,)), dma((share // 2,)), dma((share,)),
            dma((chips,)), dma((chips,)), dma((chips,)), dma((chips,)),
        ],
        compiler_params=pltpu.CompilerParams(
            collective_id=0, has_side_effects=True, vmem_limit_bytes=44 * 1024 * 1024
        ),
        name="surrogate_kernel",
    )(tokens, gain.reshape(1, -1), up, down, head)


def local(
    tile_tokens, norm_gain, up_weight, down_weight, head_weight,
    source_index, source_cutoff, source_weight,
):
    groups = lax.axis_size("src")
    mine = lax.axis_index("src")
    ff = up_weight.shape[1]
    quarter = ff // groups
    wide = -(-quarter // 256) * 256
    up = lax.dynamic_slice_in_dim(up_weight, mine * quarter, quarter, 1)
    up = jnp.pad(up, ((0, 0), (0, wide - quarter)))
    coeffs = surrogate(
        tile_tokens, norm_gain, up, down_weight, head_weight, lax.axis_size("tile"), groups
    )
    return image(coeffs, source_index, source_cutoff, source_weight)


def solution(mesh):
    return jax.shard_map(
        local,
        mesh=mesh,
        in_specs=(
            P(("tile", "src"), None), P(), P("tile", None), P("tile", None),
            P(None, "src"), P(), P(), P(),
        ),
        out_specs=P(("tile", "src"), None),
        check_vma=False,
    )
```

```python
import functools

import jax
import jax.numpy as jnp
import ml_dtypes
import numpy as np
from jax import lax
from jax.experimental import pallas as pl
from jax.experimental.pallas import tpu as pltpu
from jax.sharding import PartitionSpec as P

GRID = 16
SUB = 8
W = 32
PIX = 64
PATCH = 256
ORD = 128
HEADW = 768


def split_two(table):
    high = table.astype(ml_dtypes.bfloat16)
    low = (table - high.astype(np.float64)).astype(ml_dtypes.bfloat16)
    return high, low


def image_tables():
    angle = 2 * np.pi * (np.outer(np.arange(ORD), np.arange(PIX)) % PIX) / PIX
    c, s = np.cos(angle), np.sin(angle)
    one = np.block([[c, s, -s, c], [-s, c, -c, -s]])
    table_one = np.concatenate(split_two(one), 1)
    angle = 2 * np.pi * (np.outer(np.arange(PIX), np.arange(W)) % PIX) / PIX
    high, low = split_two(np.concatenate([np.cos(angle), np.sin(angle)], 1))
    table_two = np.concatenate([high, low, high], 1)
    return table_one, table_two


def image_kernel(
    sources, index_ref, cutoff_ref, weight_ref, coeffs_ref, one_ref, two_ref, out_ref, spectra,
):
    row = lax.broadcasted_iota(jnp.int32, (PATCH, 2 * SUB * ORD), 0)
    lane = lax.broadcasted_iota(jnp.int32, (PATCH, 2 * SUB * ORD), 1)
    own = (row % GRID) == ((lane % ORD) // SUB)
    row, lane = row[:128], lane[:128]
    same = (row // SUB == lane // ORD) & (row % SUB == lane % SUB)
    spread = jnp.where(same, 1.0, 0.0).astype(jnp.bfloat16)
    row = lax.broadcasted_iota(jnp.int32, (GRID, PATCH), 0)
    lane = lax.broadcasted_iota(jnp.int32, (GRID, PATCH), 1)
    gather = jnp.where(row == lane // GRID, 1.0, 0.0).astype(jnp.bfloat16)
    for pair in range(6):
        wide = jnp.dot(
            coeffs_ref[:, pair * 128:(pair + 1) * 128], spread,
            preferred_element_type=jnp.float32,
        )
        kept = jnp.where(own, wide, 0.0).astype(jnp.bfloat16)
        rows = jnp.dot(gather, kept, preferred_element_type=jnp.float32)
        for part in range(2):
            for u in range(SUB):
                at = (part * SUB + u) * ORD
                spectra[2 * pair + part, pl.ds(u, GRID, stride=SUB), :] = rows[:, at:at + ORD]

    order_i = lax.broadcasted_iota(jnp.int32, (W, ORD), 0) - W // 2
    order_j = lax.broadcasted_iota(jnp.int32, (W, ORD), 1) - W // 2

    def add_source(s, total):
        x0 = index_ref[2 * s]
        y0 = index_ref[2 * s + 1]
        radius = cutoff_ref[s]
        col = order_j - y0
        inside = (order_i * order_i + col * col <= radius * radius) & (col < W // 2)
        window = spectra[:, pl.ds(x0, W), :]
        window = jnp.where(inside[None], window, 0.0)
        both = jnp.concatenate(
            [jnp.concatenate([window[2 * k], window[2 * k + 1]], 1) for k in range(6)], 0
        ).astype(jnp.bfloat16)
        half = jnp.dot(both, one_ref[...], preferred_element_type=jnp.float32)
        half = half[:, :256] + half[:, 256:]
        high = half.astype(jnp.bfloat16)
        low = (half - high.astype(jnp.float32)).astype(jnp.bfloat16)

        def stacked(part):
            return jnp.concatenate(
                [
                    jnp.concatenate(
                        [part[k * W:(k + 1) * W, :128], part[k * W:(k + 1) * W, 128:]], 0
                    )
                    for k in range(6)
                ],
                1,
            )

        high, low = stacked(high), stacked(low)
        field = jnp.dot(
            two_ref[...], jnp.concatenate([high, high, low], 0),
            preferred_element_type=jnp.float32,
        )
        field = field * field
        power = field[:, :128]
        for k in range(1, 6):
            power = power + field[:, k * 128:(k + 1) * 128]
        return total + weight_ref[s] * power

    total = lax.fori_loop(0, sources, add_source, jnp.zeros((PIX, 128), jnp.float32), unroll=8)
    out_ref[...] = (total[:, :PIX] + total[:, PIX:]) * (1.0 / (6.0 * W * W * sources))


def image(coeffs, source_index, source_cutoff, source_weight):
    sources = source_weight.shape[0]
    smem = pl.BlockSpec(memory_space=pltpu.SMEM)
    vmem = pl.BlockSpec(memory_space=pltpu.VMEM)
    tables = [jnp.asarray(t) for t in image_tables()]
    out = pl.pallas_call(
        functools.partial(image_kernel, sources),
        out_shape=jax.ShapeDtypeStruct((PIX, PIX), jnp.float32),
        in_specs=[smem] * 3 + [vmem] * 3,
        out_specs=vmem,
        scratch_shapes=[pltpu.VMEM((12, ORD, ORD), jnp.float32)],
        compiler_params=pltpu.CompilerParams(vmem_limit_bytes=24 * 1024 * 1024),
        name="image_kernel",
    )(source_index.reshape(-1), source_cutoff, source_weight, coeffs, *tables)
    return out.reshape(1, PIX * PIX)


MESH = pl.DeviceIdType.MESH


def surrogate_kernel(
    tiles, groups, tok_ref, gain_ref, up_ref, down_ref, head_ref, out_ref,
    tok_buf, norm_buf, up_buf, acc, block, block_in, fold_own, fold_buf, fold_all,
    part, mine_part, sib_buf, cross_out, cross_in, kept_buf,
    up_send, up_fsend, up_lsend, up_recv, tok_send, tok_fsend, tok_recv, block_send, block_recv,
    fold_send, fold_fsend, fold_lsend, fold_recv, sib_send, sib_recv, cross_send, cross_recv,
):
    t, s = lax.axis_index("tile"), lax.axis_index("src")
    tile_pairs, chips = tiles // 2, groups // 2
    side, pair = lax.rem(t, 2), t // 2
    core, chip = lax.rem(s, 2), s // 2
    width = head_ref.shape[1]
    depth = up_ref.shape[0]
    share = tiles // groups
    owner = t // share

    def send(source, target, sent, got, tile, col):
        return pltpu.make_async_remote_copy(
            src_ref=source, dst_ref=target, send_sem=sent, recv_sem=got,
            device_id={"tile": tile, "src": col}, device_id_type=MESH,
        )

    def tile_at(k):
        return 2 * lax.rem(pair + k, tile_pairs) + side

    def line(step):
        return (pair + step >= 0) & (pair + step < tile_pairs)

    def col_at(k):
        return 2 * lax.rem(chip + k, chips) + core

    tile_mate = t + 1 - 2 * side
    col_mate = s + 1 - 2 * core

    barrier = pltpu.get_barrier_semaphore()
    for step in (-1, 1):
        @pl.when(line(step))
        def _():
            pl.semaphore_signal(
                barrier, inc=1, device_id={"tile": t + 2 * step, "src": s}, device_id_type=MESH
            )
    pl.semaphore_signal(barrier, inc=1, device_id={"tile": tile_mate, "src": s}, device_id_type=MESH)
    for k in range(1, groups):
        pl.semaphore_signal(
            barrier, inc=1, device_id={"tile": t, "src": lax.rem(s + k, groups)}, device_id_type=MESH
        )
    pl.semaphore_wait(barrier, groups + line(-1).astype(jnp.int32) + line(1).astype(jnp.int32))

    up_mate = send(up_ref, up_buf.at[t], up_send.at[0], up_recv.at[t], tile_mate, s)
    up_line = {
        step: send(up_ref, up_buf.at[t], up_send.at[(3 + step) // 2], up_recv.at[t], t + 2 * step, s)
        for step in (-1, 1)
    }
    tok_copies = [
        send(tok_ref, tok_buf.at[s], tok_send.at[k], tok_recv.at[s], t, col_mate if k == 0 else col_at(k))
        for k in range(chips)
    ]
    for step in (-1, 1):
        @pl.when(line(step))
        def _():
            up_line[step].start()
    for copy in tok_copies[1:] + [up_mate] + tok_copies[:1]:
        copy.start()

    block[...] = jnp.dot(
        down_ref[...], head_ref[...], preferred_element_type=jnp.float32
    ).astype(jnp.bfloat16)
    block_copy = send(block, block_in.at[s], block_send, block_recv.at[s], t, owner)

    @pl.when(s != owner)
    def _():
        block_copy.start()

    def normalise(source, col):
        value = source[...].astype(jnp.float32)
        square = jnp.mean(value * value, axis=1, keepdims=True)
        value = (value * lax.rsqrt(square + 1e-05) * gain_ref[...]).astype(jnp.bfloat16)
        for j in range(tiles):
            norm_buf[j, col] = value[:, j * depth:(j + 1) * depth]

    def keep(source, col):
        kept = jnp.dot(source[...], head_ref[...], preferred_element_type=jnp.float32)
        kept_buf[col] = jnp.zeros(kept_buf.shape[1:], jnp.float32)
        for q in range(groups):
            @pl.when(s == q)
            def _():
                kept_buf[col, :, q * width:(q + 1) * width] = kept

    own_fold = lax.rem(t, share)
    fold_mate = send(
        fold_own, fold_buf.at[own_fold], fold_send.at[0], fold_recv.at[own_fold], tile_mate, s
    )
    fold_line = {
        step: send(
            fold_own, fold_buf.at[own_fold], fold_send.at[(3 + step) // 2],
            fold_recv.at[own_fold], t + 2 * step, s,
        )
        for step in (-1, 1)
    }

    @pl.when(s == owner)
    def _():
        for k in range(1, groups):
            col = lax.rem(s + k, groups)
            send(block, block_in.at[col], block_send, block_recv.at[col], t, s).wait_recv()
        for q in range(groups):
            @pl.when(s == q)
            def _():
                fold_own[:, q * width:(q + 1) * width] = block[...]

            @pl.when(s != q)
            def _():
                fold_own[:, q * width:(q + 1) * width] = block_in[q]

        for step in (-1, 1):
            @pl.when(line(step))
            def _():
                fold_line[step].start()
        fold_mate.start()
        fold_buf[lax.rem(t, share)] = fold_own[...]

    def up_forward(k, step):
        at = t - 2 * step * k
        return (
            send(up_buf.at[at], up_buf.at[at], up_fsend.at[at // 2], up_recv.at[at], tile_mate, s),
            send(up_buf.at[at], up_buf.at[at], up_lsend.at[at // 2], up_recv.at[at], t + 2 * step, s),
        )

    def fold_forward(j, step):
        at = 2 * j + side
        return (
            send(fold_buf.at[at], fold_buf.at[at], fold_fsend.at[j], fold_recv.at[at], tile_mate, s),
            send(fold_buf.at[at], fold_buf.at[at], fold_lsend.at[j], fold_recv.at[at], t + 2 * step, s),
        )

    def fold_pair(j):
        return s * (share // 2) + j

    def up_handle(k, act):
        for step in (1, -1):
            @pl.when(line(-step * k))
            def _():
                act(up_forward(k, step), step)

    def fold_handle(k, act):
        for j in range(share // 2):
            for step in (1, -1):
                @pl.when(pair == fold_pair(j) + step * k)
                def _():
                    act(fold_forward(j, step), step)

    def pass_on(copies, step):
        copies[0].wait_recv()

        @pl.when(line(step))
        def _():
            copies[1].start()
        copies[0].start()

    def finish(copies, step):
        copies[0].wait_send()

        @pl.when(line(step))
        def _():
            copies[1].wait_send()

    def tok_forward(k):
        at = col_at(k)
        return send(tok_buf.at[at], tok_buf.at[at], tok_fsend.at[k], tok_recv.at[at], t, col_mate)

    def add_block(rows_ref, at, cols, first=False):
        for g in cols:
            value = jnp.dot(norm_buf[at, g], rows_ref[...], preferred_element_type=jnp.float32)
            if first:
                acc[g] = value
            else:
                acc[g] = acc[g] + value

    near = [s, col_mate]
    normalise(tok_ref, s)
    for k in range(1, tile_pairs):
        up_handle(k, pass_on)
        if k > 1:
            fold_handle(k - 1, pass_on)
        if k == 1:
            send(
                tok_ref, tok_buf.at[col_mate], tok_send.at[0], tok_recv.at[col_mate], t, col_mate
            ).wait_recv()
            normalise(tok_buf.at[col_mate], col_mate)
            keep(tok_ref, s)
            add_block(up_ref, t, near, True)
    fold_handle(tile_pairs - 1, pass_on)
    for k in range(1, chips):
        tok_forward(k).wait_recv()
        tok_forward(k).start()
    keep(tok_buf.at[col_mate], col_mate)
    for k in range(1, chips):
        normalise(tok_buf.at[col_at(k)], col_at(k))
        keep(tok_buf.at[col_at(k)], col_at(k))
    far = []
    for k in range(1, chips):
        at = 2 * lax.rem(chip + k, chips) + 1 - core
        send(tok_ref, tok_buf.at[at], tok_send.at[0], tok_recv.at[at], t, col_mate).wait_recv()
        normalise(tok_buf.at[at], at)
        keep(tok_buf.at[at], at)
        far += [col_at(k), at]
    add_block(up_ref, t, far, True)
    for k in range(1, tile_pairs):
        add_block(up_buf.at[tile_at(k)], tile_at(k), near + far)
    for k in range(tile_pairs):
        for step in ((1, -1) if k else (1,)):
            @pl.when(line(-step * k))
            def _():
                at = tile_mate - 2 * step * k
                send(up_ref, up_buf.at[at], up_send.at[0], up_recv.at[at], tile_mate, s).wait_recv()
                add_block(up_buf.at[at], at, near + far)
    for j in range(share // 2):
        at = 2 * j + 1 - side
        send(fold_own, fold_buf.at[at], fold_send.at[0], fold_recv.at[at], tile_mate, s).wait_recv()
    folded = jnp.concatenate([fold_buf[j].astype(jnp.float32) for j in range(share)], 0)
    real = folded.shape[0]
    fold_all[...] = jnp.zeros_like(fold_all)
    fold_all[:real, :] = folded.astype(jnp.bfloat16)

    def partial(col, target):
        value = acc[col]
        inner = 0.7978845608028654 * (value + 0.044715 * (value * value * value))
        hidden = (0.5 * value * (1.0 + jnp.tanh(inner))).astype(jnp.bfloat16)
        target[...] = (
            jnp.dot(hidden, fold_all[...], preferred_element_type=jnp.float32) + kept_buf[col]
        )

    def sib_copy(k):
        return send(part.at[k], sib_buf.at[k], sib_send.at[k], sib_recv.at[k], t, col_mate)

    def cross_copy(k):
        return send(cross_out.at[k], cross_in.at[k], cross_send.at[k], cross_recv.at[k], t, col_at(k))

    for k in list(range(1, chips)) + [0]:
        partial(2 * lax.rem(chip + k, chips) + 1 - core, part.at[k])
        sib_copy(k).start()
        partial(col_at(k), mine_part)
        sib_copy(k).wait_recv()
        mine_part[...] += sib_buf[k]
        if k > 0:
            cross_out[k] = mine_part[...].astype(jnp.bfloat16)
            cross_copy(k).start()
    total = mine_part[...]
    for k in range(1, chips):
        cross_copy(k).wait_recv()
        total = total + cross_in[k].astype(jnp.float32)
    out_ref[...] = total.astype(jnp.bfloat16)

    for copy in [up_mate] + tok_copies:
        copy.wait_send()
    for step in (-1, 1):
        @pl.when(line(step))
        def _():
            up_line[step].wait_send()
    for k in range(1, tile_pairs):
        up_handle(k, finish)
        fold_handle(k, finish)
    for k in range(1, chips):
        tok_forward(k).wait_send()
        cross_copy(k).wait_send()
    for k in range(chips):
        sib_copy(k).wait_send()

    @pl.when(s != owner)
    def _():
        block_copy.wait_send()

    @pl.when(s == owner)
    def _():
        fold_mate.wait_send()
        for step in (-1, 1):
            @pl.when(line(step))
            def _():
                fold_line[step].wait_send()


def surrogate(tokens, gain, up, down, head, tiles, groups):
    rows, model = tokens.shape
    depth, wide = up.shape
    ff_rows, width = down.shape[0], head.shape[1]
    outs = groups * width
    share, chips = tiles // groups, groups // 2
    dma = pltpu.SemaphoreType.DMA
    bf16, f32 = jnp.bfloat16, jnp.float32
    vmem = pl.BlockSpec(memory_space=pltpu.VMEM)
    return pl.pallas_call(
        functools.partial(surrogate_kernel, tiles, groups),
        out_shape=jax.ShapeDtypeStruct((rows, outs), bf16),
        in_specs=[vmem] * 5,
        out_specs=vmem,
        scratch_shapes=[
            pltpu.VMEM((groups, rows, model), bf16),
            pltpu.VMEM((tiles, groups, rows, depth), bf16),
            pltpu.VMEM((tiles, depth, wide), bf16),
            pltpu.VMEM((groups, rows, wide), f32),
            pltpu.VMEM((ff_rows, width), bf16),
            pltpu.VMEM((groups, ff_rows, width), bf16),
            pltpu.VMEM((ff_rows, outs), bf16),
            pltpu.VMEM((share, ff_rows, outs), bf16),
            pltpu.VMEM((wide, outs), bf16),
            pltpu.VMEM((chips, rows, outs), f32),
            pltpu.VMEM((rows, outs), f32),
            pltpu.VMEM((chips, rows, outs), f32),
            pltpu.VMEM((chips, rows, outs), bf16),
            pltpu.VMEM((chips, rows, outs), bf16),
            pltpu.VMEM((groups, rows, outs), f32),
            dma((3,)), dma((tiles // 2,)), dma((tiles // 2,)), dma((tiles,)),
            dma((chips,)), dma((chips,)), dma((groups,)),
            dma(()), dma((groups,)),
            dma((3,)), dma((share // 2,)), dma((share // 2,)), dma((share,)),
            dma((chips,)), dma((chips,)), dma((chips,)), dma((chips,)),
        ],
        compiler_params=pltpu.CompilerParams(
            collective_id=0, has_side_effects=True, vmem_limit_bytes=44 * 1024 * 1024
        ),
        name="surrogate_kernel",
    )(tokens, gain.reshape(1, -1), up, down, head)


def local(
    tile_tokens, norm_gain, up_weight, down_weight, head_weight,
    source_index, source_cutoff, source_weight,
):
    groups = lax.axis_size("src")
    mine = lax.axis_index("src")
    ff = up_weight.shape[1]
    quarter = ff // groups
    wide = -(-quarter // 256) * 256
    up = lax.dynamic_slice_in_dim(up_weight, mine * quarter, quarter, 1)
    up = jnp.pad(up, ((0, 0), (0, wide - quarter)))
    coeffs = surrogate(
        tile_tokens, norm_gain, up, down_weight, head_weight, lax.axis_size("tile"), groups
    )
    return image(coeffs, source_index, source_cutoff, source_weight)


def solution(mesh):
    return jax.shard_map(
        local,
        mesh=mesh,
        in_specs=(
            P(("tile", "src"), None), P(), P("tile", None), P("tile", None),
            P(None, "src"), P(), P(), P(),
        ),
        out_specs=P(("tile", "src"), None),
        check_vma=False,
    )
```

```python
import functools

import jax
import jax.numpy as jnp
import ml_dtypes
import numpy as np
from jax import lax
from jax.experimental import pallas as pl
from jax.experimental.pallas import tpu as pltpu
from jax.sharding import PartitionSpec as P

GRID = 16
SUB = 8
W = 32
PIX = 64
PATCH = 256
ORD = 128
HEADW = 768


def split_two(table):
    high = table.astype(ml_dtypes.bfloat16)
    low = (table - high.astype(np.float64)).astype(ml_dtypes.bfloat16)
    return high, low


def image_tables():
    angle = 2 * np.pi * (np.outer(np.arange(ORD), np.arange(PIX)) % PIX) / PIX
    c, s = np.cos(angle), np.sin(angle)
    one = np.block([[c, s, -s, c], [-s, c, -c, -s]])
    table_one = np.concatenate(split_two(one), 1)
    angle = 2 * np.pi * (np.outer(np.arange(PIX), np.arange(W)) % PIX) / PIX
    high, low = split_two(np.concatenate([np.cos(angle), np.sin(angle)], 1))
    table_two = np.concatenate([high, low, high], 1)
    return table_one, table_two


def image_kernel(
    sources, index_ref, cutoff_ref, weight_ref, coeffs_ref, one_ref, two_ref, out_ref, spectra,
):
    row = lax.broadcasted_iota(jnp.int32, (PATCH, 2 * SUB * ORD), 0)
    lane = lax.broadcasted_iota(jnp.int32, (PATCH, 2 * SUB * ORD), 1)
    own = (row % GRID) == ((lane % ORD) // SUB)
    row, lane = row[:128], lane[:128]
    same = (row // SUB == lane // ORD) & (row % SUB == lane % SUB)
    spread = jnp.where(same, 1.0, 0.0).astype(jnp.bfloat16)
    row = lax.broadcasted_iota(jnp.int32, (GRID, PATCH), 0)
    lane = lax.broadcasted_iota(jnp.int32, (GRID, PATCH), 1)
    gather = jnp.where(row == lane // GRID, 1.0, 0.0).astype(jnp.bfloat16)
    for pair in range(6):
        wide = jnp.dot(
            coeffs_ref[:, pair * 128:(pair + 1) * 128], spread,
            preferred_element_type=jnp.float32,
        )
        kept = jnp.where(own, wide, 0.0).astype(jnp.bfloat16)
        rows = jnp.dot(gather, kept, preferred_element_type=jnp.float32)
        for part in range(2):
            for u in range(SUB):
                at = (part * SUB + u) * ORD
                spectra[2 * pair + part, pl.ds(u, GRID, stride=SUB), :] = rows[:, at:at + ORD]

    order_i = lax.broadcasted_iota(jnp.int32, (W, ORD), 0) - W // 2
    order_j = lax.broadcasted_iota(jnp.int32, (W, ORD), 1) - W // 2

    def add_source(s, total):
        x0 = index_ref[s, 0]
        y0 = index_ref[s, 1]
        radius = cutoff_ref[s]
        col = order_j - y0
        inside = (order_i * order_i + col * col <= radius * radius) & (col < W // 2)
        window = spectra[:, pl.ds(x0, W), :]
        window = jnp.where(inside[None], window, 0.0)
        both = jnp.concatenate(
            [jnp.concatenate([window[2 * k], window[2 * k + 1]], 1) for k in range(6)], 0
        ).astype(jnp.bfloat16)
        half = jnp.dot(both, one_ref[...], preferred_element_type=jnp.float32)
        half = half[:, :256] + half[:, 256:]
        high = half.astype(jnp.bfloat16)
        low = (half - high.astype(jnp.float32)).astype(jnp.bfloat16)

        def stacked(part):
            return jnp.concatenate(
                [
                    jnp.concatenate(
                        [part[k * W:(k + 1) * W, :128], part[k * W:(k + 1) * W, 128:]], 0
                    )
                    for k in range(6)
                ],
                1,
            )

        high, low = stacked(high), stacked(low)
        field = jnp.dot(
            two_ref[...], jnp.concatenate([high, high, low], 0),
            preferred_element_type=jnp.float32,
        )
        field = field * field
        power = field[:, :128]
        for k in range(1, 6):
            power = power + field[:, k * 128:(k + 1) * 128]
        return total + weight_ref[s] * power

    total = lax.fori_loop(0, sources, add_source, jnp.zeros((PIX, 128), jnp.float32), unroll=8)
    total = (total[:, :PIX] + total[:, PIX:]) * (1.0 / (6.0 * W * W * sources))
    for x in range(0, PIX, 2):
        out_ref[:, x * PIX:(x + 2) * PIX] = jnp.concatenate([total[x:x + 1], total[x + 1:x + 2]], 1)


def image(coeffs, source_index, source_cutoff, source_weight):
    sources = source_weight.shape[0]
    smem = pl.BlockSpec(memory_space=pltpu.SMEM)
    vmem = pl.BlockSpec(memory_space=pltpu.VMEM)
    tables = [jnp.asarray(t) for t in image_tables()]
    return pl.pallas_call(
        functools.partial(image_kernel, sources),
        out_shape=jax.ShapeDtypeStruct((1, PIX * PIX), jnp.float32),
        in_specs=[smem] * 3 + [vmem] * 3,
        out_specs=vmem,
        scratch_shapes=[pltpu.VMEM((12, ORD, ORD), jnp.float32)],
        compiler_params=pltpu.CompilerParams(vmem_limit_bytes=24 * 1024 * 1024),
        name="image_kernel",
    )(source_index, source_cutoff, source_weight, coeffs, *tables)


MESH = pl.DeviceIdType.MESH


def surrogate_kernel(
    tiles, groups, tok_ref, gain_ref, up_ref, down_ref, head_ref, out_ref,
    tok_buf, norm_buf, up_buf, acc, block, block_in, fold_own, fold_buf, fold_all,
    part, mine_part, sib_buf, cross_out, cross_in, kept_buf,
    up_send, up_fsend, up_lsend, up_recv, tok_send, tok_fsend, tok_recv, block_send, block_recv,
    fold_send, fold_fsend, fold_lsend, fold_recv, sib_send, sib_recv, cross_send, cross_recv,
):
    t, s = lax.axis_index("tile"), lax.axis_index("src")
    tile_pairs, chips = tiles // 2, groups // 2
    side, pair = lax.rem(t, 2), t // 2
    core, chip = lax.rem(s, 2), s // 2
    width = head_ref.shape[1]
    depth = up_ref.shape[0]
    share = tiles // groups
    owner = t // share

    def send(source, target, sent, got, tile, col):
        return pltpu.make_async_remote_copy(
            src_ref=source, dst_ref=target, send_sem=sent, recv_sem=got,
            device_id={"tile": tile, "src": col}, device_id_type=MESH,
        )

    def tile_at(k):
        return 2 * lax.rem(pair + k, tile_pairs) + side

    def line(step):
        return (pair + step >= 0) & (pair + step < tile_pairs)

    def col_at(k):
        return 2 * lax.rem(chip + k, chips) + core

    tile_mate = t + 1 - 2 * side
    col_mate = s + 1 - 2 * core

    barrier = pltpu.get_barrier_semaphore()
    for step in (-1, 1):
        @pl.when(line(step))
        def _():
            pl.semaphore_signal(
                barrier, inc=1, device_id={"tile": t + 2 * step, "src": s}, device_id_type=MESH
            )
    pl.semaphore_signal(barrier, inc=1, device_id={"tile": tile_mate, "src": s}, device_id_type=MESH)
    for k in range(1, groups):
        pl.semaphore_signal(
            barrier, inc=1, device_id={"tile": t, "src": lax.rem(s + k, groups)}, device_id_type=MESH
        )
    pl.semaphore_wait(barrier, groups + line(-1).astype(jnp.int32) + line(1).astype(jnp.int32))

    up_mate = send(up_ref, up_buf.at[t], up_send.at[0], up_recv.at[t], tile_mate, s)
    up_line = {
        step: send(up_ref, up_buf.at[t], up_send.at[(3 + step) // 2], up_recv.at[t], t + 2 * step, s)
        for step in (-1, 1)
    }
    tok_copies = [
        send(tok_ref, tok_buf.at[s], tok_send.at[k], tok_recv.at[s], t, col_mate if k == 0 else col_at(k))
        for k in range(chips)
    ]
    for step in (-1, 1):
        @pl.when(line(step))
        def _():
            up_line[step].start()
    for copy in tok_copies[1:] + [up_mate] + tok_copies[:1]:
        copy.start()

    block[...] = jnp.dot(
        down_ref[...], head_ref[...], preferred_element_type=jnp.float32
    ).astype(jnp.bfloat16)
    block_copy = send(block, block_in.at[s], block_send, block_recv.at[s], t, owner)

    @pl.when(s != owner)
    def _():
        block_copy.start()

    def normalise(source, col):
        value = source[...].astype(jnp.float32)
        square = jnp.mean(value * value, axis=1, keepdims=True)
        value = (value * lax.rsqrt(square + 1e-05) * gain_ref[...]).astype(jnp.bfloat16)
        for j in range(tiles):
            norm_buf[j, col] = value[:, j * depth:(j + 1) * depth]

    def keep(source, col):
        kept = jnp.dot(source[...], head_ref[...], preferred_element_type=jnp.float32)
        kept_buf[col] = jnp.zeros(kept_buf.shape[1:], jnp.float32)
        for q in range(groups):
            @pl.when(s == q)
            def _():
                kept_buf[col, :, q * width:(q + 1) * width] = kept

    own_fold = lax.rem(t, share)
    fold_mate = send(
        fold_own, fold_buf.at[own_fold], fold_send.at[0], fold_recv.at[own_fold], tile_mate, s
    )
    fold_line = {
        step: send(
            fold_own, fold_buf.at[own_fold], fold_send.at[(3 + step) // 2],
            fold_recv.at[own_fold], t + 2 * step, s,
        )
        for step in (-1, 1)
    }

    @pl.when(s == owner)
    def _():
        for k in range(1, groups):
            col = lax.rem(s + k, groups)
            send(block, block_in.at[col], block_send, block_recv.at[col], t, s).wait_recv()
        for q in range(groups):
            @pl.when(s == q)
            def _():
                fold_own[:, q * width:(q + 1) * width] = block[...]

            @pl.when(s != q)
            def _():
                fold_own[:, q * width:(q + 1) * width] = block_in[q]

        for step in (-1, 1):
            @pl.when(line(step))
            def _():
                fold_line[step].start()
        fold_mate.start()
        fold_buf[lax.rem(t, share)] = fold_own[...]

    def up_forward(k, step):
        at = t - 2 * step * k
        return (
            send(up_buf.at[at], up_buf.at[at], up_fsend.at[at // 2], up_recv.at[at], tile_mate, s),
            send(up_buf.at[at], up_buf.at[at], up_lsend.at[at // 2], up_recv.at[at], t + 2 * step, s),
        )

    def fold_forward(j, step):
        at = 2 * j + side
        return (
            send(fold_buf.at[at], fold_buf.at[at], fold_fsend.at[j], fold_recv.at[at], tile_mate, s),
            send(fold_buf.at[at], fold_buf.at[at], fold_lsend.at[j], fold_recv.at[at], t + 2 * step, s),
        )

    def fold_pair(j):
        return s * (share // 2) + j

    def up_handle(k, act):
        for step in (1, -1):
            @pl.when(line(-step * k))
            def _():
                act(up_forward(k, step), step)

    def fold_handle(k, act):
        for j in range(share // 2):
            for step in (1, -1):
                @pl.when(pair == fold_pair(j) + step * k)
                def _():
                    act(fold_forward(j, step), step)

    def pass_on(copies, step):
        copies[0].wait_recv()

        @pl.when(line(step))
        def _():
            copies[1].start()
        copies[0].start()

    def finish(copies, step):
        copies[0].wait_send()

        @pl.when(line(step))
        def _():
            copies[1].wait_send()

    def tok_forward(k):
        at = col_at(k)
        return send(tok_buf.at[at], tok_buf.at[at], tok_fsend.at[k], tok_recv.at[at], t, col_mate)

    def add_block(rows_ref, at, cols, first=False):
        for g in cols:
            value = jnp.dot(norm_buf[at, g], rows_ref[...], preferred_element_type=jnp.float32)
            if first:
                acc[g] = value
            else:
                acc[g] = acc[g] + value

    near = [s, col_mate]
    normalise(tok_ref, s)
    for k in range(1, tile_pairs):
        up_handle(k, pass_on)
        if k > 1:
            fold_handle(k - 1, pass_on)
        if k == 1:
            send(
                tok_ref, tok_buf.at[col_mate], tok_send.at[0], tok_recv.at[col_mate], t, col_mate
            ).wait_recv()
            normalise(tok_buf.at[col_mate], col_mate)
            keep(tok_ref, s)
            add_block(up_ref, t, near, True)
    fold_handle(tile_pairs - 1, pass_on)
    for k in range(1, chips):
        tok_forward(k).wait_recv()
        tok_forward(k).start()
    keep(tok_buf.at[col_mate], col_mate)
    for k in range(1, chips):
        normalise(tok_buf.at[col_at(k)], col_at(k))
        keep(tok_buf.at[col_at(k)], col_at(k))
    far = []
    for k in range(1, chips):
        at = 2 * lax.rem(chip + k, chips) + 1 - core
        send(tok_ref, tok_buf.at[at], tok_send.at[0], tok_recv.at[at], t, col_mate).wait_recv()
        normalise(tok_buf.at[at], at)
        keep(tok_buf.at[at], at)
        far += [col_at(k), at]
    add_block(up_ref, t, far, True)
    for k in range(1, tile_pairs):
        add_block(up_buf.at[tile_at(k)], tile_at(k), near + far)
    for k in range(tile_pairs):
        for step in ((1, -1) if k else (1,)):
            @pl.when(line(-step * k))
            def _():
                at = tile_mate - 2 * step * k
                send(up_ref, up_buf.at[at], up_send.at[0], up_recv.at[at], tile_mate, s).wait_recv()
                add_block(up_buf.at[at], at, near + far)
    for j in range(share // 2):
        at = 2 * j + 1 - side
        send(fold_own, fold_buf.at[at], fold_send.at[0], fold_recv.at[at], tile_mate, s).wait_recv()
    folded = jnp.concatenate([fold_buf[j].astype(jnp.float32) for j in range(share)], 0)
    real = folded.shape[0]
    fold_all[...] = jnp.zeros_like(fold_all)
    fold_all[:real, :] = folded.astype(jnp.bfloat16)

    def partial(col, target):
        value = acc[col]
        inner = 0.7978845608028654 * (value + 0.044715 * (value * value * value))
        hidden = (0.5 * value * (1.0 + jnp.tanh(inner))).astype(jnp.bfloat16)
        target[...] = (
            jnp.dot(hidden, fold_all[...], preferred_element_type=jnp.float32) + kept_buf[col]
        )

    def sib_copy(k):
        return send(part.at[k], sib_buf.at[k], sib_send.at[k], sib_recv.at[k], t, col_mate)

    def cross_copy(k):
        return send(cross_out.at[k], cross_in.at[k], cross_send.at[k], cross_recv.at[k], t, col_at(k))

    for k in list(range(1, chips)) + [0]:
        partial(2 * lax.rem(chip + k, chips) + 1 - core, part.at[k])
        sib_copy(k).start()
        partial(col_at(k), mine_part)
        sib_copy(k).wait_recv()
        mine_part[...] += sib_buf[k]
        if k > 0:
            cross_out[k] = mine_part[...].astype(jnp.bfloat16)
            cross_copy(k).start()
    total = mine_part[...]
    for k in range(1, chips):
        cross_copy(k).wait_recv()
        total = total + cross_in[k].astype(jnp.float32)
    out_ref[...] = total.astype(jnp.bfloat16)

    for copy in [up_mate] + tok_copies:
        copy.wait_send()
    for step in (-1, 1):
        @pl.when(line(step))
        def _():
            up_line[step].wait_send()
    for k in range(1, tile_pairs):
        up_handle(k, finish)
        fold_handle(k, finish)
    for k in range(1, chips):
        tok_forward(k).wait_send()
        cross_copy(k).wait_send()
    for k in range(chips):
        sib_copy(k).wait_send()

    @pl.when(s != owner)
    def _():
        block_copy.wait_send()

    @pl.when(s == owner)
    def _():
        fold_mate.wait_send()
        for step in (-1, 1):
            @pl.when(line(step))
            def _():
                fold_line[step].wait_send()


def surrogate(tokens, gain, up, down, head, tiles, groups):
    rows, model = tokens.shape
    depth, wide = up.shape
    ff_rows, width = down.shape[0], head.shape[1]
    outs = groups * width
    share, chips = tiles // groups, groups // 2
    dma = pltpu.SemaphoreType.DMA
    bf16, f32 = jnp.bfloat16, jnp.float32
    vmem = pl.BlockSpec(memory_space=pltpu.VMEM)
    return pl.pallas_call(
        functools.partial(surrogate_kernel, tiles, groups),
        out_shape=jax.ShapeDtypeStruct((rows, outs), bf16),
        in_specs=[vmem] * 5,
        out_specs=vmem,
        scratch_shapes=[
            pltpu.VMEM((groups, rows, model), bf16),
            pltpu.VMEM((tiles, groups, rows, depth), bf16),
            pltpu.VMEM((tiles, depth, wide), bf16),
            pltpu.VMEM((groups, rows, wide), f32),
            pltpu.VMEM((ff_rows, width), bf16),
            pltpu.VMEM((groups, ff_rows, width), bf16),
            pltpu.VMEM((ff_rows, outs), bf16),
            pltpu.VMEM((share, ff_rows, outs), bf16),
            pltpu.VMEM((wide, outs), bf16),
            pltpu.VMEM((chips, rows, outs), f32),
            pltpu.VMEM((rows, outs), f32),
            pltpu.VMEM((chips, rows, outs), f32),
            pltpu.VMEM((chips, rows, outs), bf16),
            pltpu.VMEM((chips, rows, outs), bf16),
            pltpu.VMEM((groups, rows, outs), f32),
            dma((3,)), dma((tiles // 2,)), dma((tiles // 2,)), dma((tiles,)),
            dma((chips,)), dma((chips,)), dma((groups,)),
            dma(()), dma((groups,)),
            dma((3,)), dma((share // 2,)), dma((share // 2,)), dma((share,)),
            dma((chips,)), dma((chips,)), dma((chips,)), dma((chips,)),
        ],
        compiler_params=pltpu.CompilerParams(
            collective_id=0, has_side_effects=True, vmem_limit_bytes=44 * 1024 * 1024
        ),
        name="surrogate_kernel",
    )(tokens, gain.reshape(1, -1), up, down, head)


def local(
    tile_tokens, norm_gain, up_weight, down_weight, head_weight,
    source_index, source_cutoff, source_weight,
):
    groups = lax.axis_size("src")
    mine = lax.axis_index("src")
    ff = up_weight.shape[1]
    quarter = ff // groups
    wide = -(-quarter // 256) * 256
    up = lax.dynamic_slice_in_dim(up_weight, mine * quarter, quarter, 1)
    up = jnp.pad(up, ((0, 0), (0, wide - quarter)))
    coeffs = surrogate(
        tile_tokens, norm_gain, up, down_weight, head_weight, lax.axis_size("tile"), groups
    )
    return image(coeffs, source_index, source_cutoff, source_weight)


def solution(mesh):
    return jax.shard_map(
        local,
        mesh=mesh,
        in_specs=(
            P(("tile", "src"), None), P(), P("tile", None), P("tile", None),
            P(None, "src"), P(), P(), P(),
        ),
        out_specs=P(("tile", "src"), None),
        check_vma=False,
    )
```
